1024 devices in a mesh: domain: 32 (over x, y, core), member: 32 (over z).
Axes of the slice: x: 4, y: 4, z: 32, core: 2. Of those that a mesh axis runs over, the one named last changes fastest.
Arguments:
- state: bfloat16 [256, 2048, 256], P('member', 'domain'), may hold values from -6 to 6
- obs_ens: bfloat16 [256, 65536], P('member', 'domain'), may hold values from -6 to 6
- y_obs: bfloat16 [65536], P('domain'), may hold values from -12 to 12
- obs_rinv: bfloat16 [65536], P('domain'), may hold values from 0.29882812 to 3
- block_list: int32 [2048, 8], P('domain'), may hold values from 0 to 1023, as said below
- loc_class: int32 [2048, 8], P('domain'), may hold values from 0 to 7
- loc_table: float32 [8], replicated, may hold values from 0.1 to 1
- patch_active: int32 [2048], P('domain'), may hold values from 0 to 1, as said below
Outputs:
- analysis: bfloat16 [256, 2048, 256], P('member', 'domain')
The draws below stay inside these ranges and needn't reach their ends.
Inputs may be any that keep to these rules, and one draw needn't show every extreme that they name: `block_list`: the 8 blocks of a patch are distinct, and for a patch of domain group g (patches g * 64 to (g + 1) * 64 - 1) they lie among blocks g * 32 - 6 to (g + 1) * 32 + 5. `patch_active`: exactly 32 of the 64 patches of each domain group are 1.
All inputs are finite; a program needn't handle non-finite values.
Results may differ from the reference program's by a relative error of at most 0.015.
Values may be sent and summed in bfloat16 or wider, within the bound.
A program may use at most 32 MiB of HBM per device.

```python
import math
import jax
import jax.numpy as jnp
from jax import lax

MEMBERS = 256
NS = 256
BROWS = 64
BPP = 8
HB = 6
BLK_DOM = 32
NCLASS = 8
NEWTON = 6
PAT_DOM = 64
ACT = 32
PATCHES = 2048
NBLOCKS = 1024
OBS_ROWS = 512
N_DOMAIN = 32


def draw_block_list(key, part):
    patches = jnp.arange(PATCHES, dtype=jnp.int32)
    groups = patches // PAT_DOM
    position = patches % PAT_DOM
    center = groups * BLK_DOM + position * BLK_DOM // PAT_DOM
    start = jnp.clip(center - HB, 0, NBLOCKS - (2 * HB + 1))
    keys = jax.random.split(jax.random.fold_in(key, 11), PATCHES)
    ends = jnp.array([0, 2 * HB], dtype=jnp.int32)

    def one_list(single):
        middle = (jax.random.permutation(single, 2 * HB - 1)[:BPP - 2] + 1).astype(jnp.int32)
        return jnp.concatenate([ends, middle])
    offsets = jax.vmap(one_list)(keys)
    return (start[:, None] + offsets).astype(jnp.int32)


def draw_patch_active(key, part):
    groups = PATCHES // PAT_DOM
    keys = jax.random.split(jax.random.fold_in(key, 23), groups)
    ranks = jax.vmap(lambda single: jax.random.permutation(single, PAT_DOM))(keys)
    return (ranks < ACT).astype(jnp.int32).reshape(PATCHES)


def set_ends(result, stream_key, least, largest):
    spot = [jax.random.randint(jax.random.fold_in(stream_key, axis), (), 0, length) for axis, length in enumerate(result.shape)]
    main_axis = result.shape.index(max(result.shape))
    next_to = spot[:main_axis] + [(spot[main_axis] + 1) % result.shape[main_axis]] + spot[main_axis + 1:]
    return result.at[tuple(spot)].set(least).at[tuple(next_to)].set(largest)


def block_scale(stream_key, dims, pieces, smallest, high):
    gain, own = 1.0, jax.random.fold_in(stream_key, 6)
    for dim, parts in pieces:
        steps = jnp.exp(jax.random.uniform(jax.random.fold_in(own, dim), (parts,), jnp.float32, smallest / len(pieces), high / len(pieces)))
        gain = gain * jnp.repeat(steps, dims[dim] // parts).reshape([-1 if axis == dim else 1 for axis in range(len(dims))])
    return gain


def bell_draw(rng, shape, deviation, most, shards=(), kind=jnp.bfloat16):
    level = block_scale(rng, shape, shards, -0.22, 0.18) if shards else 1.0
    values = jax.random.normal(rng, shape, jnp.float32) * deviation * level
    return jnp.minimum(jnp.maximum(values, -most), most).astype(kind)


def setup_inputs(seed: int = 0) -> dict:
    seeds = jax.random.split(jax.random.key(seed), 9)
    state = bell_draw(seeds[0], (MEMBERS, PATCHES, NS), 1.0, 6.0, ((0, 32), (1, 32)))
    obs_ens = bell_draw(seeds[1], (MEMBERS, NBLOCKS * BROWS), 1.0, 6.0, ((0, 32), (1, 32)))
    y_obs = bell_draw(seeds[2], (NBLOCKS * BROWS,), 3.0, 12.0, ((0, 32),))
    obs_rinv = jnp.clip(jnp.exp(math.log(3.0) - 2.306499 * jax.random.uniform(seeds[3], (NBLOCKS * BROWS,), jnp.float32) ** block_scale(seeds[3], (NBLOCKS * BROWS,), ((0, 32),), -0.2, 0.2)), 0.29882812, 3.0).astype(jnp.bfloat16)
    block_list = draw_block_list(jax.random.fold_in(seeds[8], 71), 0)
    loc_class = set_ends(jax.random.randint(seeds[5], (PATCHES, BPP), 0, NCLASS), jax.random.fold_in(seeds[5], 1), 0, NCLASS - 1).astype(jnp.int32)
    loc_table = jnp.clip(jnp.exp(jax.random.uniform(seeds[6], (NCLASS,), jnp.float32, math.log(0.1), math.log(1.0))), 0.1, 1.0)
    patch_active = draw_patch_active(jax.random.fold_in(seeds[8], 71), 0)
    return {"state": state, "obs_ens": obs_ens, "y_obs": y_obs, "obs_rinv": obs_rinv, "block_list": block_list, "loc_class": loc_class, "loc_table": loc_table, "patch_active": patch_active}


def analyse_patch(obs_sel, y_sel, rinv_sel, loc_rows, members_state):
    count = obs_sel.shape[0]
    ones_row = jnp.ones((count,), jnp.bfloat16)
    obs_mean = jnp.dot(ones_row, obs_sel, preferred_element_type=jnp.float32) / count
    obs_pert = (obs_sel - obs_mean).astype(jnp.bfloat16)
    row_weight = rinv_sel.astype(jnp.float32) * loc_rows
    weighted = (obs_pert * row_weight).astype(jnp.bfloat16)
    gram = lax.dot_general(weighted, obs_pert, (((1,), (1,)), ((), ())), preferred_element_type=jnp.float32)
    identity = jnp.eye(count, dtype=jnp.float32)
    system = identity + gram / (count - 1)
    innovation = y_sel.astype(jnp.float32) - obs_mean
    projected = jnp.dot(weighted.astype(jnp.float32), innovation, precision=lax.Precision.HIGHEST)
    frobenius = jnp.sqrt(jnp.sum(system * system))
    iter_y = system / frobenius
    iter_z = identity
    for step in range(NEWTON):
        halfway = 1.5 * identity - 0.5 * jnp.dot(iter_z, iter_y, precision=lax.Precision.HIGHEST)
        iter_y = jnp.dot(iter_y, halfway, precision=lax.Precision.HIGHEST)
        iter_z = jnp.dot(halfway, iter_z, precision=lax.Precision.HIGHEST)
    inner = jnp.dot(iter_z, projected, precision=lax.Precision.HIGHEST)
    mean_weight = jnp.dot(iter_z, inner, precision=lax.Precision.HIGHEST) / (frobenius * (count - 1))
    transform = (iter_z / jnp.sqrt(frobenius) + mean_weight[:, None]).astype(jnp.bfloat16)
    state_mean = jnp.dot(ones_row, members_state, preferred_element_type=jnp.float32) / count
    state_pert = (members_state - state_mean).astype(jnp.bfloat16)
    update = lax.dot_general(transform, state_pert, (((0,), (0,)), ((), ())), preferred_element_type=jnp.float32)
    return (state_mean + update).astype(jnp.bfloat16)

def reference(state, obs_ens, y_obs, obs_rinv, block_list, loc_class, loc_table, patch_active):
    classes = jnp.arange(loc_table.shape[0], dtype=jnp.int32)
    loc_weight = lax.optimization_barrier(jnp.sum(jnp.where(loc_class[..., None] == classes, loc_table, jnp.float32(0.0)), axis=-1))
    obs_blocks = obs_ens.reshape(MEMBERS, NBLOCKS, BROWS)
    y_blocks = y_obs.reshape(NBLOCKS, BROWS)
    rinv_blocks = obs_rinv.reshape(NBLOCKS, BROWS)
    grouped = (1 - patch_active).reshape(N_DOMAIN, PAT_DOM)
    ordering = jnp.argsort(grouped, axis=1, stable=True)[:, :ACT].astype(jnp.int32)
    offsets = (jnp.arange(N_DOMAIN, dtype=jnp.int32) * PAT_DOM)[:, None]
    chosen = (ordering + offsets).reshape(-1).astype(jnp.int32)

    def one_patch(patch):
        listed = block_list[patch]
        obs_sel = obs_blocks[:, listed].reshape(MEMBERS, OBS_ROWS)
        y_sel = y_blocks[listed].reshape(OBS_ROWS)
        rinv_sel = rinv_blocks[listed].reshape(OBS_ROWS)
        loc_rows = jnp.repeat(loc_weight[patch], BROWS)
        members_state = lax.dynamic_index_in_dim(state, patch, 1, keepdims=False)
        return analyse_patch(obs_sel, y_sel, rinv_sel, loc_rows, members_state)
    analysed = lax.map(one_patch, chosen)
    return state.at[:, chosen].set(jnp.transpose(analysed, (1, 0, 2)))
```

```python
import jax
import jax.numpy as jnp
from jax import lax
from jax.experimental import pallas as pl
from jax.experimental.pallas import tpu as pltpu
from jax.sharding import PartitionSpec as P

MESH = pl.DeviceIdType.MESH
F32 = jnp.float32
BF16 = jnp.bfloat16
N = 32
MEM = 8
NS = 256
BROWS = 64
BPP = 8
HB = 6
BLK_DOM = 32
PAT = 64
ROWS = BPP * BROWS
HALO = HB * BROWS
WIDTH = BLK_DOM * BROWS
TILES = (WIDTH + 2 * HALO) // 128
COUNT = N * MEM
NEWTON = 6
STACK = 16
FAR_FIRST = [16] + [s for k in range(15, 0, -1) for s in (k, N - k)]
EARLY = 11


def iota(shape, dim):
    return lax.broadcasted_iota(jnp.int32, shape, dim)


def dot(a, b):
    return jnp.dot(a, b, preferred_element_type=F32)


def split(a):
    high = a.astype(BF16)
    return high, (a - high.astype(F32)).astype(BF16)


def dot3(a, b):
    return dot(a[0], b[0]) + (dot(a[0], b[1]) + dot(a[1], b[0]))


def flat(ref):
    value = ref[...].astype(F32)
    return value.reshape(value.shape[0] * value.shape[1], value.shape[2])


def slabs(value):
    return value.reshape(N, MEM, value.shape[-1]).astype(BF16)


def analyse(obs, yr, loc_rows, y_it, z_it):
    mean = jnp.sum(obs, axis=0, keepdims=True) / COUNT
    pert = (obs - mean).astype(BF16)
    weight = yr[1:2] * loc_rows
    weighted = (pert.astype(F32) * weight).astype(BF16)
    gram = lax.dot_general(weighted, pert, (((1,), (1,)), ((), ())), preferred_element_type=F32)
    eye = (iota((COUNT, COUNT), 0) == iota((COUNT, COUNT), 1)).astype(F32)
    system = eye + gram / (COUNT - 1)
    projected = jnp.sum(weighted.astype(F32) * (yr[0:1] - mean), axis=1, keepdims=True)
    squares = jnp.sum(jnp.sum(system * system, axis=0, keepdims=True), axis=1, keepdims=True)
    fro = jnp.sqrt(squares)
    first = system / fro
    half = 1.5 * eye - 0.5 * first
    y_it[...] = dot3(split(first), split(half))
    z_it[...] = half

    def step(_, carry):
        y, z = split(y_it[...]), split(z_it[...])
        middle = split(1.5 * eye - 0.5 * dot3(z, y))
        y_it[...] = dot3(y, middle)
        z_it[...] = dot3(middle, z)
        return carry

    lax.fori_loop(0, NEWTON - 2, step, 0)
    y, z = split(y_it[...]), split(z_it[...])
    last = dot3(split(1.5 * eye - 0.5 * dot3(z, y)), z)
    z = split(last)
    inner = dot3(z, split(jnp.broadcast_to(projected, (COUNT, COUNT))))
    shift = dot3(z, split(inner)) / (fro * (COUNT - 1))
    return (last / jnp.sqrt(fro) + shift).astype(BF16)


def kernel(
    state_ref, stack_ref, list_ref, class_ref, active_ref, table_ref, out_ref,
    ext, send_o, recv_o, send_s, recv_s, send_r, recv_r, choose, y_it, z_it,
    so_sem, ro_sem, ss_sem, rs_sem, sr_sem, rr_sem, hs_sem, hr_sem,
):
    group, me = lax.axis_index("domain"), lax.axis_index("member")
    right, left = lax.rem(group + 1, N), lax.rem(group + N - 1, N)

    barrier = pltpu.get_barrier_semaphore()
    for k in FAR_FIRST:
        pl.semaphore_signal(
            barrier, inc=1, device_id={"member": lax.rem(me + k, N)}, device_id_type=MESH
        )
    for side in (left, right):
        pl.semaphore_signal(barrier, inc=1, device_id={"domain": side}, device_id_type=MESH)

    def push(src, dst, send_sem, recv_sem, order):
        for k in order:
            peer = lax.rem(me + k, N)
            pltpu.make_async_remote_copy(
                src_ref=src.at[peer], dst_ref=dst.at[me], send_sem=send_sem, recv_sem=recv_sem,
                device_id={"member": peer}, device_id_type=MESH,
            ).start()

    def own(src, dst, recv_sem):
        pltpu.make_async_copy(src.at[me], dst.at[me], recv_sem).start()

    def arrived(dst, recv_sem):
        pltpu.make_async_copy(dst, dst, recv_sem).wait()

    def sent(src, send_sem):
        part = src.at[pl.ds(0, N - 1)]
        pltpu.make_async_copy(part, part, send_sem).wait()

    act = active_ref[...].astype(F32)
    act8 = jnp.broadcast_to(act, (8, PAT))
    wide = (PAT, MEM * PAT)
    upto = (iota(wide, 0) <= iota(wide, 1) % PAT).astype(F32)
    same = (iota(wide, 0) == iota(wide, 1) % PAT).astype(F32)
    rank = dot(act8, upto)[0:1] - 1.0
    live = dot(act8, same)[0:1]
    rank = jnp.where(live > 0.5, rank, -1.0).astype(jnp.int32)
    big = (COUNT, MEM * PAT)
    pick = (rank == iota(big, 0) // MEM) & (iota(big, 1) // PAT == iota(big, 0) % MEM)
    choose[...] = pick.astype(F32).astype(BF16)
    send_s[...] = slabs(dot(choose[...], state_ref[...]))
    ext[:, HALO:HALO + WIDTH] = stack_ref[...]

    ids = (list_ref[...] - (group * BLK_DOM - HB)).astype(F32).astype(BF16)
    rank64 = rank[:, :PAT]
    rows64 = (rank64 == iota((COUNT, PAT), 0) // MEM).astype(F32).astype(BF16)
    listed = dot(rows64, ids).astype(jnp.int32)
    mine = (rank64 == jnp.broadcast_to(me, (8, PAT))).astype(F32).astype(BF16)
    listed_mine = dot(mine, ids).astype(jnp.int32)
    classes = dot(mine, class_ref[...].astype(F32).astype(BF16)).astype(jnp.int32)
    weights = jnp.zeros(classes.shape, F32)
    for c in range(8):
        weights = jnp.where(classes == c, table_ref[c], weights)
    lane = iota((1, ROWS), 1) // BROWS
    loc_rows = jnp.zeros((1, ROWS), F32)
    for b in range(BPP):
        loc_rows = jnp.where(lane == b, weights[0:1, b:b + 1], loc_rows)

    pl.semaphore_wait(barrier, N + 1)

    to_right = pltpu.make_async_remote_copy(
        src_ref=stack_ref.at[:, pl.ds(WIDTH - HALO, HALO)], dst_ref=ext.at[:, pl.ds(0, HALO)],
        send_sem=hs_sem.at[0], recv_sem=hr_sem.at[0],
        device_id={"domain": right}, device_id_type=MESH,
    )
    to_left = pltpu.make_async_remote_copy(
        src_ref=stack_ref.at[:, pl.ds(0, HALO)], dst_ref=ext.at[:, pl.ds(HALO + WIDTH, HALO)],
        send_sem=hs_sem.at[1], recv_sem=hr_sem.at[1],
        device_id={"domain": left}, device_id_type=MESH,
    )
    to_right.start()
    to_left.start()
    own(send_s, recv_s, rs_sem)
    push(send_s, recv_s, ss_sem, rs_sem, FAR_FIRST[:EARLY])
    to_right.wait_recv()
    to_left.wait_recv()

    straight = jnp.concatenate([ext[:, t * 128:(t + 1) * 128] for t in range(TILES)], axis=0)
    turn = (iota((128, 128), 0) == (iota((128, 128), 1) + BROWS) % 128).astype(F32).astype(BF16)
    turned = dot(straight, turn).astype(BF16)
    table = jnp.concatenate([straight, turned], axis=0)
    half_tile = iota((1, 128), 1) < BROWS

    def gather(ids_of, row_in_stack):
        shape = (ids_of.shape[0], 2 * TILES * STACK)
        tiles = []
        for pair in range(BPP // 2):
            sides = []
            for b in (2 * pair, 2 * pair + 1):
                block = ids_of[:, b:b + 1]
                key = (((block + b) & 1) * TILES + (block >> 1)) * STACK + row_in_stack
                hot = (iota(shape, 1) == key).astype(F32).astype(BF16)
                sides.append(dot(hot, table))
            tiles.append(jnp.where(half_tile, sides[0], sides[1]))
        return tiles

    for pair, tile in enumerate(gather(listed, iota((COUNT, 1), 0) % MEM)):
        send_o[:, :, pair * 128:(pair + 1) * 128] = slabs(tile)
    own(send_o, recv_o, ro_sem)
    push(send_o, recv_o, so_sem, ro_sem, FAR_FIRST)
    push(send_s, recv_s, ss_sem, rs_sem, FAR_FIRST[EARLY:])
    yr = jnp.concatenate(gather(listed_mine, MEM + iota((8, 1), 0)), axis=1)

    arrived(recv_o, ro_sem)
    transform = analyse(flat(recv_o), yr, loc_rows, y_it, z_it)
    arrived(recv_s, rs_sem)
    members = flat(recv_s)
    mean = jnp.sum(members, axis=0, keepdims=True) / COUNT
    update = lax.dot_general(
        transform, (members - mean).astype(BF16), (((0,), (0,)), ((), ())),
        preferred_element_type=F32,
    )
    send_r[...] = slabs(mean + update)
    own(send_r, recv_r, rr_sem)
    push(send_r, recv_r, sr_sem, rr_sem, FAR_FIRST)

    across = (((0,), (0,)), ((), ()))
    ones = jnp.ones((COUNT, NS), BF16)
    analysed = lax.dot_general(choose[...], ones, across, preferred_element_type=F32) > 0.5
    to_right.wait_send()
    to_left.wait_send()
    sent(send_s, ss_sem)
    sent(send_o, so_sem)
    arrived(recv_r, rr_sem)
    back = lax.dot_general(
        choose[...], flat(recv_r).astype(BF16), across, preferred_element_type=F32
    )
    out_ref[...] = jnp.where(analysed, back, state_ref[...].astype(F32)).astype(BF16)
    sent(send_r, sr_sem)


def per_device(state, obs_ens, y_obs, obs_rinv, block_list, loc_class, loc_table, patch_active):
    stack = jnp.concatenate(
        [obs_ens, y_obs[None, :], obs_rinv[None, :], jnp.zeros((STACK - MEM - 2, WIDTH), BF16)],
        axis=0,
    )
    vmem = pl.BlockSpec(memory_space=pltpu.VMEM)
    out = pl.pallas_call(
        kernel,
        out_shape=jax.ShapeDtypeStruct((MEM * PAT, NS), BF16),
        in_specs=[vmem] * 5 + [pl.BlockSpec(memory_space=pltpu.SMEM)],
        out_specs=vmem,
        scratch_shapes=[
            pltpu.VMEM((STACK, WIDTH + 2 * HALO), BF16),
            pltpu.VMEM((N, MEM, ROWS), BF16),
            pltpu.VMEM((N, MEM, ROWS), BF16),
            pltpu.VMEM((N, MEM, NS), BF16),
            pltpu.VMEM((N, MEM, NS), BF16),
            pltpu.VMEM((N, MEM, NS), BF16),
            pltpu.VMEM((N, MEM, NS), BF16),
            pltpu.VMEM((COUNT, MEM * PAT), BF16),
            pltpu.VMEM((COUNT, COUNT), F32),
            pltpu.VMEM((COUNT, COUNT), F32),
        ]
        + [pltpu.SemaphoreType.DMA(())] * 6
        + [pltpu.SemaphoreType.DMA((2,))] * 2,
        compiler_params=pltpu.CompilerParams(
            collective_id=0, has_side_effects=True, vmem_limit_bytes=32 * 1024 * 1024
        ),
        cost_estimate=pl.CostEstimate(
            flops=4_000_000_000, bytes_accessed=2_000_000, transcendentals=0
        ),
    )(
        state.reshape(MEM * PAT, NS), stack, block_list, loc_class,
        patch_active[None, :], loc_table,
    )
    return out.reshape(MEM, PAT, NS)


def solution(mesh):
    placed = (
        P("member", "domain", None),
        P("member", "domain"),
        P("domain"),
        P("domain"),
        P("domain", None),
        P("domain", None),
        P(),
        P("domain"),
    )
    return jax.shard_map(
        per_device,
        mesh=mesh,
        in_specs=placed,
        out_specs=P("member", "domain", None),
        check_vma=False,
    )
```

```python
import jax
import jax.numpy as jnp
from jax import lax
from jax.experimental import pallas as pl
from jax.experimental.pallas import tpu as pltpu
from jax.sharding import PartitionSpec as P

MESH = pl.DeviceIdType.MESH
F32 = jnp.float32
BF16 = jnp.bfloat16
N = 32
MEM = 8
NS = 256
BROWS = 64
BPP = 8
HB = 6
BLK_DOM = 32
PAT = 64
ROWS = BPP * BROWS
HALO = HB * BROWS
WIDTH = BLK_DOM * BROWS
SIDE = HALO + 256
MAIN = 256 + WIDTH + 256 + 256
TILES = (WIDTH + 2 * HALO) // 128
COUNT = N * MEM
NEWTON = 6
FAR_FIRST = [16] + [s for k in range(15, 0, -1) for s in (k, N - k)]
NT = (((1,), (1,)), ((), ()))
TN = (((0,), (0,)), ((), ()))


def iota(shape, dim):
    return lax.broadcasted_iota(jnp.int32, shape, dim)


def dot(a, b):
    return jnp.dot(a, b, preferred_element_type=F32)


def split(a):
    high = a.astype(BF16)
    return high, (a - high.astype(F32)).astype(BF16)


def dot3(a, b):
    return dot(a[0], b[0]) + (dot(a[0], b[1]) + dot(a[1], b[0]))


def flat(ref):
    value = ref[...].astype(F32)
    return value.reshape(value.shape[0] * value.shape[1], value.shape[2])


def slabs(value):
    return value.reshape(N, MEM, value.shape[-1]).astype(BF16)


def analyse(obs, yr, loc_rows, y_it, z_it):
    mean = jnp.sum(obs, axis=0, keepdims=True) / COUNT
    pert = (obs - mean).astype(BF16)
    weight = yr[1:2] * loc_rows
    weighted = (pert.astype(F32) * weight).astype(BF16)
    gram = lax.dot_general(weighted, pert, (((1,), (1,)), ((), ())), preferred_element_type=F32)
    eye = (iota((COUNT, COUNT), 0) == iota((COUNT, COUNT), 1)).astype(F32)
    system = eye + gram / (COUNT - 1)
    projected = jnp.sum(weighted.astype(F32) * (yr[0:1] - mean), axis=1, keepdims=True)
    squares = jnp.sum(jnp.sum(system * system, axis=0, keepdims=True), axis=1, keepdims=True)
    fro = jnp.sqrt(squares)
    first = system / fro
    half = 1.5 * eye - 0.5 * first
    y_it[...] = dot3(split(first), split(half))
    z_it[...] = half

    def step(_, carry):
        y, z = split(y_it[...]), split(z_it[...])
        middle = split(1.5 * eye - 0.5 * dot3(z, y))
        y_it[...] = dot3(y, middle)
        z_it[...] = dot3(middle, z)
        return carry

    lax.fori_loop(0, NEWTON - 2, step, 0)
    y, z = split(y_it[...]), split(z_it[...])
    last = dot3(split(1.5 * eye - 0.5 * dot3(z, y)), z)
    z = split(last)
    inner = dot3(z, split(jnp.broadcast_to(projected, (COUNT, COUNT))))
    shift = dot3(z, split(inner)) / (fro * (COUNT - 1))
    return (last / jnp.sqrt(fro) + shift).astype(BF16)


def level(group):
    return group // 2 + (N // 2) * (group % 2)


def group_of(lev):
    return 2 * (lev % (N // 2)) + lev // (N // 2)


def ranks(active):
    square = (PAT, PAT)
    upto = (iota(square, 0) <= iota(square, 1)).astype(F32)
    return jnp.where(active > 0.5, dot(active, upto) - 1.0, -1.0)


def kernel(
    state_hbm, obs_hbm, y_hbm, rinv_hbm, list_hbm, class_hbm, active_hbm, table_ref, out_ref,
    state, y_in, rinv_in, list_in, class_in, active_in,
    msg, main, before, after, send_o, recv_o, send_s, relay, recv_s, send_r, recv_r,
    choose, y_it, z_it,
    in_sem, msg_send, msg_recv, so_sem, ro_sem, s1_sem, r1_sem, s2_sem, r2_sem, sr_sem, rr_sem,
):
    group, me = lax.axis_index("domain"), lax.axis_index("member")
    place = level(group)
    served = group_of(me)

    def where_to(dom, mem):
        return {"domain": dom, "member": mem}

    def is_self(dom, mem):
        return (dom == group) & (mem == me)

    inputs = [
        pltpu.make_async_copy(src, dst, in_sem.at[i])
        for i, (src, dst) in enumerate(
            [
                (obs_hbm, msg.at[:, pl.ds(256, WIDTH)]),
                (y_hbm, y_in),
                (rinv_hbm, rinv_in),
                (list_hbm, list_in),
                (class_hbm, class_in),
                (active_hbm, active_in),
                (state_hbm, state),
            ]
        )
    ]
    for copy in inputs:
        copy.start()

    up, down = lax.rem(group + 1, N), lax.rem(group + N - 1, N)
    served_up, served_down = lax.rem(served + 1, N), lax.rem(served + N - 1, N)
    edge = 256 + WIDTH - HALO
    messages = [
        (msg, main, (me, place), (served, group)),
        (msg.at[:, pl.ds(edge, SIDE)], before, (me, level(up)), (served_down, group)),
        (msg.at[:, pl.ds(0, SIDE)], after, (me, level(down)), (served_up, group)),
    ]

    barrier = pltpu.get_barrier_semaphore()
    for k in FAR_FIRST:
        pl.semaphore_signal(
            barrier, inc=1, device_id=where_to(group, lax.rem(me + k, N)), device_id_type=MESH
        )
    for _, _, _, source in messages:

        @pl.when(jnp.logical_not(is_self(*source)))
        def _(source=source):
            pl.semaphore_signal(barrier, inc=1, device_id=where_to(*source), device_id_type=MESH)

    for k in range(1, N):
        pl.semaphore_signal(
            barrier, inc=1, device_id=where_to(lax.rem(group + k, N), me), device_id_type=MESH
        )

    def remote(src, dst, send_sem, recv_sem, target):
        return pltpu.make_async_remote_copy(
            src_ref=src, dst_ref=dst, send_sem=send_sem, recv_sem=recv_sem,
            device_id=where_to(*target), device_id_type=MESH,
        )

    def arrived(dst, recv_sem):
        pltpu.make_async_copy(dst, dst, recv_sem).wait()

    def sent(src, send_sem):
        part = src.at[pl.ds(0, N - 1)]
        pltpu.make_async_copy(part, part, send_sem).wait()

    for copy in inputs[1:6]:
        copy.wait()
    active = jnp.broadcast_to(active_in[...].astype(F32), (8, PAT))
    y_rows, rinv_rows = y_in[...].astype(F32), rinv_in[...].astype(F32)
    msg[:, 0:128] = y_rows[0:8].astype(BF16)
    msg[:, 128:256] = rinv_rows[0:8].astype(BF16)
    msg[:, 256 + WIDTH:384 + WIDTH] = y_rows[8:16].astype(BF16)
    msg[:, 384 + WIDTH:512 + WIDTH] = rinv_rows[8:16].astype(BF16)
    local_ids = (list_in[...] - (group * BLK_DOM - HB)).astype(F32)
    meta = jnp.concatenate([local_ids, class_in[...].astype(F32)], axis=1)
    msg[:, 512 + WIDTH:640 + WIDTH] = meta.astype(BF16)
    msg[:, 640 + WIDTH:768 + WIDTH] = jnp.concatenate([active, active], axis=1).astype(BF16)
    inputs[0].wait()

    big = (COUNT, MEM * PAT)
    rank = ranks(active)[0:1]
    rank = jnp.concatenate([rank] * MEM, axis=1).astype(jnp.int32)
    pick = (rank == iota(big, 0) // MEM) & (iota(big, 1) // PAT == iota(big, 0) % MEM)
    choose[...] = pick.astype(F32).astype(BF16)
    inputs[6].wait()
    send_s[...] = slabs(dot(choose[...], state[...]))

    peers = 2 * (N - 1)
    for _, _, target, _ in messages:
        peers = peers + jnp.where(is_self(*target), 0, 1).astype(jnp.int32)
    pl.semaphore_wait(barrier, peers)

    for i, (src, dst, target, _) in enumerate(messages):

        @pl.when(jnp.logical_not(is_self(*target)))
        def _(src=src, dst=dst, target=target, i=i):
            remote(src, dst, msg_send.at[i], msg_recv.at[i], target).start()

        @pl.when(is_self(*target))
        def _(src=src, dst=dst, i=i):
            pltpu.make_async_copy(src, dst, msg_recv.at[i]).start()

    pltpu.make_async_copy(send_s.at[group], relay.at[group], r1_sem).start()
    for k in range(1, N):
        to = lax.rem(group + k, N)
        remote(send_s.at[to], relay.at[group], s1_sem, r1_sem, (to, me)).start()
    arrived(relay, r1_sem)
    for k in FAR_FIRST:
        to = lax.rem(me + k, N)
        remote(relay.at[group_of(to)], recv_s.at[me], s2_sem, r2_sem, (group, to)).start()
    pltpu.make_async_copy(relay.at[served], recv_s.at[me], r2_sem).start()

    for i, (_, dst, _, _) in enumerate(messages):
        arrived(dst, msg_recv.at[i])
    head = ranks(main[:, 640 + WIDTH:704 + WIDTH].astype(F32))[0:1].astype(jnp.int32)
    meta = main[:, 512 + WIDTH:640 + WIDTH].astype(F32)
    ids, kinds = meta[:, 0:PAT].astype(BF16), meta[:, PAT:2 * PAT].astype(BF16)
    rows = (head == iota((COUNT, PAT), 0) // MEM).astype(F32).astype(BF16)
    listed = lax.dot_general(rows, ids, NT, preferred_element_type=F32).astype(jnp.int32)
    mine = (head == jnp.broadcast_to(group, (8, PAT))).astype(F32).astype(BF16)
    listed_mine = lax.dot_general(mine, ids, NT, preferred_element_type=F32).astype(jnp.int32)
    classes = lax.dot_general(mine, kinds, NT, preferred_element_type=F32).astype(jnp.int32)

    turn = (iota((128, 128), 0) == (iota((128, 128), 1) + BROWS) % 128).astype(F32).astype(BF16)
    half_tile = iota((1, 128), 1) < BROWS

    def both(pieces):
        straight = jnp.concatenate([piece.astype(F32) for piece in pieces], axis=0)
        turned = dot(straight.astype(BF16), turn)
        return jnp.concatenate([straight, turned], axis=0).astype(BF16)

    def gather(table, ids_of, key_of):
        shape = (ids_of.shape[0], table.shape[0])
        tiles = []
        for pair in range(BPP // 2):
            sides = []
            for b in (2 * pair, 2 * pair + 1):
                block = ids_of[:, b:b + 1]
                key = key_of((block + b) & 1, block >> 1)
                hot = (iota(shape, 1) == key).astype(F32).astype(BF16)
                sides.append(dot(hot, table))
            tiles.append(jnp.where(half_tile, sides[0], sides[1]))
        return tiles

    near = HALO // 128
    table = both(
        [before[:, t * 128:(t + 1) * 128] for t in range(near)]
        + [main[:, 256 + t * 128:384 + t * 128] for t in range(WIDTH // 128)]
        + [after[:, 256 + t * 128:384 + t * 128] for t in range(near)]
    )
    member = iota((COUNT, 1), 0) % MEM
    found = gather(table, listed, lambda turned, tile: (turned * TILES + tile) * MEM + member)
    for pair, tile in enumerate(found):
        send_o[:, :, pair * 128:(pair + 1) * 128] = slabs(tile)
    pltpu.make_async_copy(send_o.at[group], recv_o.at[group], ro_sem).start()
    for k in range(1, N):
        to = lax.rem(group + k, N)
        remote(send_o.at[to], recv_o.at[group], so_sem, ro_sem, (to, me)).start()

    values = both(
        [
            piece
            for at in (0, 128)
            for piece in (
                before[:, HALO + at:HALO + at + 128],
                main[:, at:at + 128],
                main[:, 256 + WIDTH + at:384 + WIDTH + at],
                after[:, at:at + 128],
            )
        ]
    )
    which = iota((8, 1), 0) % 2
    yr = jnp.concatenate(
        gather(
            values, listed_mine,
            lambda turned, tile: (turned * 2 + which) * 32 + tile + (8 - near),
        ),
        axis=1,
    )
    weights = jnp.zeros(classes.shape, F32)
    for c in range(8):
        weights = jnp.where(classes == c, table_ref[c], weights)
    lane = iota((1, ROWS), 1) // BROWS
    loc_rows = jnp.zeros((1, ROWS), F32)
    for b in range(BPP):
        loc_rows = jnp.where(lane == b, weights[0:1, b:b + 1], loc_rows)

    arrived(recv_o, ro_sem)
    transform = analyse(flat(recv_o), yr, loc_rows, y_it, z_it)
    arrived(recv_s, r2_sem)
    members = flat(recv_s)
    mean = jnp.sum(members, axis=0, keepdims=True) / COUNT
    update = lax.dot_general(
        transform, (members - mean).astype(BF16), TN, preferred_element_type=F32
    )
    send_r[...] = slabs(mean + update)
    for k in FAR_FIRST:
        to = lax.rem(me + k, N)
        remote(send_r.at[to], recv_r.at[group], sr_sem, rr_sem, (served, to)).start()
    home = served == group
    last = remote(send_r.at[me], recv_r.at[group], sr_sem, rr_sem, (served, me))

    @pl.when(jnp.logical_not(home))
    def _():
        last.start()

    @pl.when(home)
    def _():
        pltpu.make_async_copy(send_r.at[me], recv_r.at[group], rr_sem).start()

    ones = jnp.ones((COUNT, NS), BF16)
    analysed = lax.dot_general(choose[...], ones, TN, preferred_element_type=F32) > 0.5
    for i, (src, _, target, _) in enumerate(messages):

        @pl.when(jnp.logical_not(is_self(*target)))
        def _(src=src, i=i):
            pltpu.make_async_copy(src, src, msg_send.at[i]).wait()

    sent(send_s, s1_sem)
    sent(relay, s2_sem)
    sent(send_o, so_sem)
    arrived(recv_r, rr_sem)
    back = lax.dot_general(
        choose[...], flat(recv_r).astype(BF16), TN, preferred_element_type=F32
    )
    out_ref[...] = jnp.where(analysed, back, state[...].astype(F32)).astype(BF16)
    sent(send_r, sr_sem)

    @pl.when(jnp.logical_not(home))
    def _():
        one = send_r.at[0]
        pltpu.make_async_copy(one, one, sr_sem).wait()


def per_device(state, obs_ens, y_obs, obs_rinv, block_list, loc_class, loc_table, patch_active):
    hbm = pl.BlockSpec(memory_space=pltpu.HBM)
    slab = pltpu.VMEM((N, MEM, NS), BF16)
    wide = pltpu.VMEM((N, MEM, ROWS), BF16)
    out = pl.pallas_call(
        kernel,
        out_shape=jax.ShapeDtypeStruct((MEM * PAT, NS), BF16),
        in_specs=[hbm] * 7 + [pl.BlockSpec(memory_space=pltpu.SMEM)],
        out_specs=pl.BlockSpec(memory_space=pltpu.VMEM),
        scratch_shapes=[
            pltpu.VMEM((MEM * PAT, NS), BF16),
            pltpu.VMEM((16, 128), BF16),
            pltpu.VMEM((16, 128), BF16),
            pltpu.VMEM((BPP, PAT), jnp.int32),
            pltpu.VMEM((BPP, PAT), jnp.int32),
            pltpu.VMEM((1, PAT), jnp.int32),
            pltpu.VMEM((MEM, MAIN), BF16),
            pltpu.VMEM((MEM, MAIN), BF16),
            pltpu.VMEM((MEM, SIDE), BF16),
            pltpu.VMEM((MEM, SIDE), BF16),
            wide, wide, slab, slab, slab, slab, slab,
            pltpu.VMEM((COUNT, MEM * PAT), BF16),
            pltpu.VMEM((COUNT, COUNT), F32),
            pltpu.VMEM((COUNT, COUNT), F32),
            pltpu.SemaphoreType.DMA((7,)),
            pltpu.SemaphoreType.DMA((3,)),
            pltpu.SemaphoreType.DMA((3,)),
        ]
        + [pltpu.SemaphoreType.DMA(())] * 8,
        compiler_params=pltpu.CompilerParams(
            collective_id=0, has_side_effects=True, vmem_limit_bytes=56 * 1024 * 1024
        ),
        cost_estimate=pl.CostEstimate(
            flops=4_000_000_000, bytes_accessed=2_000_000, transcendentals=0
        ),
    )(
        state.reshape(MEM * PAT, NS), obs_ens, y_obs.reshape(16, 128), obs_rinv.reshape(16, 128),
        block_list.T, loc_class.T, patch_active[None, :], loc_table,
    )
    return out.reshape(MEM, PAT, NS)


def solution(mesh):
    placed = (
        P("member", "domain", None),
        P("member", "domain"),
        P("domain"),
        P("domain"),
        P("domain", None),
        P("domain", None),
        P(),
        P("domain"),
    )
    return jax.shard_map(
        per_device,
        mesh=mesh,
        in_specs=placed,
        out_specs=P("member", "domain", None),
        check_vma=False,
    )
```

```python
import jax
import jax.numpy as jnp
from jax import lax
from jax.experimental import pallas as pl
from jax.experimental.pallas import tpu as pltpu
from jax.sharding import PartitionSpec as P

MESH = pl.DeviceIdType.MESH
F32 = jnp.float32
BF16 = jnp.bfloat16
N = 32
MEM = 8
NS = 256
BROWS = 64
BPP = 8
HB = 6
BLK_DOM = 32
PAT = 64
ROWS = BPP * BROWS
HALO = HB * BROWS
WIDTH = BLK_DOM * BROWS
COUNT = N * MEM
NEWTON = 6
CUT = BROWS // N
SLAB = 128
EDGE = CUT * HB
OWN = CUT * BLK_DOM
Y_AT = OWN + 2 * EDGE
R_AT, ID_AT, KIND_AT = Y_AT + 1, Y_AT + 2, Y_AT + 3
FAR_FIRST = [16] + [s for k in range(15, 0, -1) for s in (k, N - k)]
NT = (((1,), (1,)), ((), ()))
TN = (((0,), (0,)), ((), ()))


def iota(shape, dim):
    return lax.broadcasted_iota(jnp.int32, shape, dim)


def dot(a, b):
    return jnp.dot(a, b, preferred_element_type=F32)


def split(a):
    high = a.astype(BF16)
    return high, (a - high.astype(F32)).astype(BF16)


def dot_dims(a, b, dims):
    return lax.dot_general(a, b, dims, preferred_element_type=F32)


def dot3(a, b, dims=(((1,), (0,)), ((), ()))):
    return dot_dims(a[0], b[0], dims) + (dot_dims(a[0], b[1], dims) + dot_dims(a[1], b[0], dims))


def one_hot(condition):
    return condition.astype(F32).astype(BF16)


def flat(ref):
    value = ref[...].astype(F32)
    return value.reshape(value.shape[0] * value.shape[1], value.shape[2])


def slabs(value):
    return value.reshape(N, MEM, value.shape[-1]).astype(BF16)


def analyse(rows, table_ref, y_it, z_it):
    obs = rows[:, :COUNT]
    mean = dot(obs.astype(BF16), jnp.ones((COUNT, COUNT), BF16)) / COUNT
    pert = (obs - mean).astype(BF16)
    kind = rows[:, COUNT + KIND_AT:COUNT + KIND_AT + 1]
    local = jnp.zeros(kind.shape, F32)
    for c in range(8):
        local = jnp.where(kind == c, table_ref[c], local)
    weight = rows[:, COUNT + R_AT:COUNT + R_AT + 1] * local
    weighted = (pert.astype(F32) * weight).astype(BF16)
    gram = dot_dims(weighted, pert, TN)
    eye = (iota((COUNT, COUNT), 0) == iota((COUNT, COUNT), 1)).astype(F32)
    system = eye + gram / (COUNT - 1)
    innovation = rows[:, COUNT + Y_AT:COUNT + Y_AT + 1] - mean
    projected = jnp.sum(weighted.astype(F32) * innovation, axis=0, keepdims=True)
    squares = jnp.sum(jnp.sum(system * system, axis=0, keepdims=True), axis=1, keepdims=True)
    fro = jnp.sqrt(squares)
    first = system / fro
    half = 1.5 * eye - 0.5 * first
    y_it[...] = dot3(split(first), split(half))
    z_it[...] = half

    def step(_, carry):
        y, z = split(y_it[...]), split(z_it[...])
        middle = split(1.5 * eye - 0.5 * dot3(z, y))
        y_it[...] = dot3(y, middle)
        z_it[...] = dot3(middle, z)
        return carry

    lax.fori_loop(0, NEWTON - 2, step, 0)
    y, z = split(y_it[...]), split(z_it[...])
    last = dot3(split(1.5 * eye - 0.5 * dot3(z, y)), z)
    z = split(last)
    inner = dot3(z, split(jnp.broadcast_to(projected, (COUNT, COUNT))), NT)
    shift = dot3(z, split(inner)) / (fro * (COUNT - 1))
    return (last / jnp.sqrt(fro) + shift).astype(BF16)


def level(group):
    return group // 2 + (N // 2) * (group % 2)


def group_of(lev):
    return 2 * (lev % (N // 2)) + lev // (N // 2)


def ranks(active):
    square = (PAT, PAT)
    upto = (iota(square, 0) <= iota(square, 1)).astype(F32)
    return jnp.where(active > 0.5, dot(active, upto) - 1.0, -1.0)


def kernel(
    state_hbm, obs_hbm, y_hbm, rinv_hbm, list_hbm, class_hbm, active_hbm, table_ref, out_ref,
    state, obs_in, y_in, rinv_in, list_in, class_in, active_in,
    send1, relay, send2, recv2, recv_s, send3, recv3, send_r, recv_r, choose, y_it, z_it,
    in_sem, s1_sem, r1_sem, s2_sem, r2_sem, ss_sem, rs_sem, s3_sem, r3_sem, sr_sem, rr_sem,
):
    group, me = lax.axis_index("domain"), lax.axis_index("member")
    served = group_of(me)

    inputs = [
        pltpu.make_async_copy(src, dst, in_sem.at[i])
        for i, (src, dst) in enumerate(
            [
                (active_hbm, active_in),
                (list_hbm, list_in),
                (class_hbm, class_in),
                (y_hbm, y_in),
                (rinv_hbm, rinv_in),
                (obs_hbm, obs_in),
                (state_hbm, state),
            ]
        )
    ]
    for copy in inputs:
        copy.start()

    barrier = pltpu.get_barrier_semaphore()
    for k in FAR_FIRST:
        to = {"domain": group, "member": lax.rem(me + k, N)}
        pl.semaphore_signal(barrier, inc=1, device_id=to, device_id_type=MESH)
    for k in range(1, N):
        to = {"domain": lax.rem(group + k, N), "member": me}
        pl.semaphore_signal(barrier, inc=1, device_id=to, device_id_type=MESH)

    def remote(src, dst, send_sem, recv_sem, dom, mem):
        return pltpu.make_async_remote_copy(
            src_ref=src, dst_ref=dst, send_sem=send_sem, recv_sem=recv_sem,
            device_id={"domain": dom, "member": mem}, device_id_type=MESH,
        )

    def arrived(dst, recv_sem):
        pltpu.make_async_copy(dst, dst, recv_sem).wait()

    def sent(src, send_sem):
        part = src.at[pl.ds(0, N - 1)]
        pltpu.make_async_copy(part, part, send_sem).wait()

    def plane(src, dst, send_sem, recv_sem):
        pltpu.make_async_copy(src.at[group], dst.at[group], recv_sem).start()
        for k in range(1, N):
            to = lax.rem(group + k, N)
            remote(src.at[to], dst.at[group], send_sem, recv_sem, to, me).start()

    def column(src_at, dst, send_sem, recv_sem):
        for k in FAR_FIRST:
            to = lax.rem(me + k, N)
            remote(src_at(group_of(to)), dst.at[me], send_sem, recv_sem, group, to).start()
        pltpu.make_async_copy(src_at(served), dst.at[me], recv_sem).start()

    for copy in inputs[:6]:
        copy.wait()
    active = jnp.broadcast_to(active_in[...].astype(F32), (8, PAT))
    rank = ranks(active)
    mine = rank == jnp.broadcast_to(me, (8, PAT)).astype(F32)
    local_ids = (list_in[...] - (group * BLK_DOM - HB)).astype(F32)
    ids = jnp.sum(jnp.where(mine, local_ids, 0.0), axis=1, keepdims=True)
    kinds = jnp.sum(jnp.where(mine, class_in[...].astype(F32), 0.0), axis=1, keepdims=True)

    square = (COUNT, 128)
    row, lane = iota(square, 0), iota(square, 1)
    member = row % MEM
    ours = (lane % BROWS) // CUT == row // MEM
    spot = (lane // BROWS) * CUT + lane % CUT
    obs = obs_in[...].astype(F32)
    parts = []
    for t in range(WIDTH // 128):
        tile = jnp.concatenate([obs[:, t * 128:(t + 1) * 128]] * N, axis=0)
        parts.append(jnp.where(ours, tile, 0.0).astype(BF16))
    narrow = (COUNT, 16)
    tile_of = one_hot(iota(narrow, 1) == 2 * (me % 8) + (iota(narrow, 0) % MEM) // 4)
    for values in (y_in, rinv_in):
        tile = dot(tile_of, values[...])
        parts.append(jnp.where(ours & (spot == member % 4), tile, 0.0).astype(BF16))
    tall = (WIDTH, SLAB)
    at = iota(tall, 0)
    goal = (at // 128) * (2 * CUT) + ((at % 128) // BROWS) * CUT + at % CUT
    place = [one_hot(iota(tall, 1) == goal)] + [one_hot(lane[:128] == a) for a in (Y_AT, R_AT)]
    packed = dot(jnp.concatenate(parts, axis=1), jnp.concatenate(place, axis=0))
    packed = jnp.where(lane == ID_AT, jnp.concatenate([ids] * N, axis=0), packed)
    packed = jnp.where(lane == KIND_AT, jnp.concatenate([kinds] * N, axis=0), packed)
    send1[:, :, 0:SLAB] = slabs(packed)

    big = (COUNT, MEM * PAT)
    wide_rank = jnp.concatenate([rank[0:1]] * MEM, axis=1).astype(jnp.int32)
    choose[...] = one_hot(
        (wide_rank == iota(big, 0) // MEM) & (iota(big, 1) // PAT == iota(big, 0) % MEM)
    )
    inputs[6].wait()
    send1[:, :, SLAB:SLAB + NS] = slabs(dot(choose[...], state[...]))

    square = (SLAB, SLAB)
    source, goal = iota(square, 0), iota(square, 1)
    plain = source == goal
    value = plain & ((goal == Y_AT) | (goal == R_AT))
    turn = me // 8
    mix = jnp.concatenate(
        [
            one_hot(
                (plain & ((goal < OWN) | (goal == ID_AT) | (goal == KIND_AT)))
                | (value & (turn == 0))
            ),
            one_hot(
                ((goal >= OWN) & (goal < OWN + EDGE) & (source == goal - EDGE))
                | (value & (turn == 1))
            ),
            one_hot(
                ((goal >= OWN + EDGE) & (goal < Y_AT) & (source == goal - OWN - EDGE))
                | (value & (turn == 2))
            ),
        ],
        axis=0,
    )

    pl.semaphore_wait(barrier, 2 * (N - 1))
    plane(send1, relay, s1_sem, r1_sem)
    arrived(relay, r1_sem)
    here = flat(relay.at[:, :, pl.ds(0, SLAB)])
    lower = jnp.concatenate([here[COUNT - MEM:], here[:COUNT - MEM]], axis=0)
    upper = jnp.concatenate([here[MEM:], here[:MEM]], axis=0)
    send2[...] = slabs(dot(jnp.concatenate([here, lower, upper], axis=1).astype(BF16), mix))
    column(lambda g: send2.at[g], recv2, s2_sem, r2_sem)
    column(lambda g: relay.at[g, :, pl.ds(SLAB, NS)], recv_s, ss_sem, rs_sem)

    arrived(recv2, r2_sem)
    held = flat(recv2)
    ids = held[:, ID_AT:ID_AT + 1].astype(jnp.int32)
    kinds = held[:, KIND_AT:KIND_AT + 1]
    held = held.astype(BF16)
    low, high = ids < HB, ids >= HB + BLK_DOM
    inner = CUT * (ids - HB)
    column_at = jnp.where(low, OWN + CUT * ids, jnp.where(high, inner + EDGE, inner))
    value_at = jnp.where(
        low, OWN + inner + OWN, jnp.where(high, inner - OWN + 2 * OWN, inner)
    )
    for cut in range(CUT):
        hot = one_hot(iota((COUNT, SLAB), 1) == column_at + cut)
        send3[:, cut, :, 0:COUNT] = slabs(dot_dims(hot, held, NT))
        hot = one_hot(iota((COUNT, COUNT), 1) == value_at + cut)
        values = jnp.where(lane == KIND_AT, kinds, dot(hot, held))
        send3[:, cut, :, COUNT:COUNT + SLAB] = slabs(values)
    plane(send3, recv3, s3_sem, r3_sem)

    arrived(recv3, r3_sem)
    rows = recv3[...].astype(F32).reshape(ROWS, COUNT + SLAB)
    transform = analyse(rows, table_ref, y_it, z_it)
    arrived(recv_s, rs_sem)
    members = flat(recv_s)
    mean = jnp.sum(members, axis=0, keepdims=True) / COUNT
    update = dot_dims(transform, (members - mean).astype(BF16), TN)
    send_r[...] = slabs(mean + update)
    for k in FAR_FIRST:
        to = lax.rem(me + k, N)
        remote(send_r.at[to], recv_r.at[group], sr_sem, rr_sem, served, to).start()
    home = served == group

    @pl.when(jnp.logical_not(home))
    def _():
        remote(send_r.at[me], recv_r.at[group], sr_sem, rr_sem, served, me).start()

    @pl.when(home)
    def _():
        pltpu.make_async_copy(send_r.at[me], recv_r.at[group], rr_sem).start()

    ones = jnp.ones((COUNT, NS), BF16)
    analysed = dot_dims(choose[...], ones, TN) > 0.5
    sent(send1, s1_sem)
    sent(send2, s2_sem)
    sent(recv_s, ss_sem)
    sent(send3, s3_sem)
    arrived(recv_r, rr_sem)
    back = dot_dims(choose[...], flat(recv_r).astype(BF16), TN)
    out_ref[...] = jnp.where(analysed, back, state[...].astype(F32)).astype(BF16)
    sent(send_r, sr_sem)

    @pl.when(jnp.logical_not(home))
    def _():
        one = send_r.at[0]
        pltpu.make_async_copy(one, one, sr_sem).wait()


def per_device(state, obs_ens, y_obs, obs_rinv, block_list, loc_class, loc_table, patch_active):
    hbm = pl.BlockSpec(memory_space=pltpu.HBM)
    slab = pltpu.VMEM((N, MEM, NS), BF16)
    out = pl.pallas_call(
        kernel,
        out_shape=jax.ShapeDtypeStruct((MEM * PAT, NS), BF16),
        in_specs=[hbm] * 7 + [pl.BlockSpec(memory_space=pltpu.SMEM)],
        out_specs=pl.BlockSpec(memory_space=pltpu.VMEM),
        scratch_shapes=[
            pltpu.VMEM((MEM * PAT, NS), BF16),
            pltpu.VMEM((MEM, WIDTH), BF16),
            pltpu.VMEM((16, 128), BF16),
            pltpu.VMEM((16, 128), BF16),
            pltpu.VMEM((BPP, PAT), jnp.int32),
            pltpu.VMEM((BPP, PAT), jnp.int32),
            pltpu.VMEM((1, PAT), jnp.int32),
            pltpu.VMEM((N, MEM, SLAB + NS), BF16),
            pltpu.VMEM((N, MEM, SLAB + NS), BF16),
            pltpu.VMEM((N, MEM, SLAB), BF16),
            pltpu.VMEM((N, MEM, SLAB), BF16),
            slab,
            pltpu.VMEM((N, CUT, MEM, COUNT + SLAB), BF16),
            pltpu.VMEM((N, CUT, MEM, COUNT + SLAB), BF16),
            slab,
            slab,
            pltpu.VMEM((COUNT, MEM * PAT), BF16),
            pltpu.VMEM((COUNT, COUNT), F32),
            pltpu.VMEM((COUNT, COUNT), F32),
            pltpu.SemaphoreType.DMA((7,)),
        ]
        + [pltpu.SemaphoreType.DMA(())] * 10,
        compiler_params=pltpu.CompilerParams(
            collective_id=0, has_side_effects=True, vmem_limit_bytes=56 * 1024 * 1024
        ),
        cost_estimate=pl.CostEstimate(
            flops=4_000_000_000, bytes_accessed=2_000_000, transcendentals=0
        ),
    )(
        state.reshape(MEM * PAT, NS), obs_ens, y_obs.reshape(16, 128), obs_rinv.reshape(16, 128),
        block_list.T, loc_class.T, patch_active[None, :], loc_table,
    )
    return out.reshape(MEM, PAT, NS)


def solution(mesh):
    placed = (
        P("member", "domain", None),
        P("member", "domain"),
        P("domain"),
        P("domain"),
        P("domain", None),
        P("domain", None),
        P(),
        P("domain"),
    )
    return jax.shard_map(
        per_device,
        mesh=mesh,
        in_specs=placed,
        out_specs=P("member", "domain", None),
        check_vma=False,
    )
```

```python
import jax
import jax.numpy as jnp
from jax import lax
from jax.experimental import pallas as pl
from jax.experimental.pallas import tpu as pltpu
from jax.sharding import PartitionSpec as P

MESH = pl.DeviceIdType.MESH
F32 = jnp.float32
BF16 = jnp.bfloat16
N = 32
MEM = 8
NS = 256
BROWS = 64
BPP = 8
HB = 6
BLK_DOM = 32
PAT = 64
ROWS = BPP * BROWS
HALO = HB * BROWS
WIDTH = BLK_DOM * BROWS
COUNT = N * MEM
NEWTON = 6
CUT = BROWS // N
SLAB = 128
EDGE = CUT * HB
OWN = CUT * BLK_DOM
Y_AT = OWN + 2 * EDGE
R_AT, ID_AT, KIND_AT = Y_AT + 1, Y_AT + 2, Y_AT + 3
SIDE = 16
FAR_FIRST = [16] + [s for k in range(15, 0, -1) for s in (k, N - k)]
STEPS = (0, 1, 2, 1)
PLANE = sorted(range(1, N), key=lambda k: -STEPS[k // 8] - STEPS[k % 8 // 2])
NT = (((1,), (1,)), ((), ()))
TN = (((0,), (0,)), ((), ()))


def iota(shape, dim):
    return lax.broadcasted_iota(jnp.int32, shape, dim)


def dot(a, b):
    return jnp.dot(a, b, preferred_element_type=F32)


def split(a):
    high = a.astype(BF16)
    return high, (a - high.astype(F32)).astype(BF16)


def dot_dims(a, b, dims):
    return lax.dot_general(a, b, dims, preferred_element_type=F32)


def dot3(a, b, dims=(((1,), (0,)), ((), ()))):
    return dot_dims(a[0], b[0], dims) + (dot_dims(a[0], b[1], dims) + dot_dims(a[1], b[0], dims))


def one_hot(condition):
    return condition.astype(F32).astype(BF16)


def flat(ref):
    value = ref[...].astype(F32)
    return value.reshape(value.shape[0] * value.shape[1], value.shape[2])


def slabs(value):
    return value.reshape(N, MEM, value.shape[-1]).astype(BF16)


def analyse(obs, values, table, y_it, z_it):
    def column_of(at, step):
        return jnp.concatenate([values[:, at + step * k:at + step * k + 1] for k in range(CUT)], 0)

    mean = dot(obs.astype(BF16), jnp.ones((COUNT, COUNT), BF16)) / COUNT
    pert = (obs - mean).astype(BF16)
    kind = column_of(KIND_AT, 0)
    local = jnp.zeros(kind.shape, F32)
    for c in range(8):
        local = jnp.where(kind == c, table[:, c:c + 1], local)
    weight = column_of(R_AT, SIDE) * local
    weighted = (pert.astype(F32) * weight).astype(BF16)
    gram = dot_dims(weighted, pert, TN)
    eye = (iota((COUNT, COUNT), 0) == iota((COUNT, COUNT), 1)).astype(F32)
    system = eye + gram / (COUNT - 1)
    innovation = column_of(Y_AT, SIDE) - mean
    projected = jnp.sum(weighted.astype(F32) * innovation, axis=0, keepdims=True)
    squares = jnp.sum(jnp.sum(system * system, axis=0, keepdims=True), axis=1, keepdims=True)
    fro = jnp.sqrt(squares)
    first = system / fro
    half = 1.5 * eye - 0.5 * first
    y_it[...] = dot3(split(first), split(half))
    z_it[...] = half

    def step(_, carry):
        y, z = split(y_it[...]), split(z_it[...])
        middle = split(1.5 * eye - 0.5 * dot3(z, y))
        y_it[...] = dot3(y, middle)
        z_it[...] = dot3(middle, z)
        return carry

    lax.fori_loop(0, NEWTON - 2, step, 0)
    y, z = split(y_it[...]), split(z_it[...])
    last = dot3(split(1.5 * eye - 0.5 * dot3(z, y)), z)
    z = split(last)
    inner = dot3(z, split(jnp.broadcast_to(projected, (COUNT, COUNT))), NT)
    shift = dot3(z, split(inner)) / (fro * (COUNT - 1))
    return (last / jnp.sqrt(fro) + shift).astype(BF16)


def level(group):
    return group // 2 + (N // 2) * (group % 2)


def group_of(lev):
    return 2 * (lev % (N // 2)) + lev // (N // 2)


def ranks(active):
    square = (PAT, PAT)
    upto = (iota(square, 0) <= iota(square, 1)).astype(F32)
    return jnp.where(active > 0.5, dot(active, upto) - 1.0, -1.0)


def kernel(
    state_hbm, obs_hbm, y_hbm, rinv_hbm, list_hbm, class_hbm, active_hbm, table_hbm, out_ref,
    state, obs_in, y_in, rinv_in, list_in, class_in, active_in, table_in,
    send1, relay, send_s, relay_s, send2, recv2, recv_s, send3, recv3, send_r, recv_r, choose, y_it, z_it,
    in_sem, s1_sem, r1_sem, sp_sem, rp_sem, s2_sem, r2_sem, ss_sem, rs_sem, s3_sem, r3_sem, sr_sem, rr_sem,
):
    group, me = lax.axis_index("domain"), lax.axis_index("member")
    served = group_of(me)

    inputs = [
        pltpu.make_async_copy(src, dst, in_sem.at[i])
        for i, (src, dst) in enumerate(
            [
                (active_hbm, active_in),
                (list_hbm, list_in),
                (class_hbm, class_in),
                (y_hbm, y_in),
                (rinv_hbm, rinv_in),
                (obs_hbm, obs_in),
                (state_hbm, state),
                (table_hbm, table_in),
            ]
        )
    ]
    for copy in inputs:
        copy.start()

    barrier = pltpu.get_barrier_semaphore()
    for k in FAR_FIRST:
        to = {"domain": group, "member": lax.rem(me + k, N)}
        pl.semaphore_signal(barrier, inc=1, device_id=to, device_id_type=MESH)
    for k in range(1, N):
        to = {"domain": lax.rem(group + k, N), "member": me}
        pl.semaphore_signal(barrier, inc=1, device_id=to, device_id_type=MESH)

    def remote(src, dst, send_sem, recv_sem, dom, mem):
        return pltpu.make_async_remote_copy(
            src_ref=src, dst_ref=dst, send_sem=send_sem, recv_sem=recv_sem,
            device_id={"domain": dom, "member": mem}, device_id_type=MESH,
        )

    def arrived(dst, recv_sem):
        pltpu.make_async_copy(dst, dst, recv_sem).wait()

    def sent(src, send_sem):
        part = src.at[pl.ds(0, N - 1)]
        pltpu.make_async_copy(part, part, send_sem).wait()

    def plane(src, dst, send_sem, recv_sem):
        pltpu.make_async_copy(src.at[group], dst.at[group], recv_sem).start()
        for k in PLANE:
            to = lax.rem(group + k, N)
            remote(src.at[to], dst.at[group], send_sem, recv_sem, to, me).start()

    def column(src_at, dst, send_sem, recv_sem):
        for k in FAR_FIRST:
            to = lax.rem(me + k, N)
            remote(src_at(group_of(to)), dst.at[me], send_sem, recv_sem, group, to).start()
        pltpu.make_async_copy(src_at(served), dst.at[me], recv_sem).start()

    for copy in inputs[:6]:
        copy.wait()
    active = jnp.broadcast_to(active_in[...].astype(F32), (8, PAT))
    rank = ranks(active)
    mine = rank == jnp.broadcast_to(me, (8, PAT)).astype(F32)
    local_ids = (list_in[...] - (group * BLK_DOM - HB)).astype(F32)
    ids = jnp.sum(jnp.where(mine, local_ids, 0.0), axis=1, keepdims=True)
    kinds = jnp.sum(jnp.where(mine, class_in[...].astype(F32), 0.0), axis=1, keepdims=True)

    square = (COUNT, 128)
    row, lane = iota(square, 0), iota(square, 1)
    member = row % MEM
    ours = (lane % BROWS) // CUT == row // MEM
    spot = (lane // BROWS) * CUT + lane % CUT
    obs = obs_in[...].astype(F32)
    parts = []
    for t in range(WIDTH // 128):
        tile = jnp.concatenate([obs[:, t * 128:(t + 1) * 128]] * N, axis=0)
        parts.append(jnp.where(ours, tile, 0.0).astype(BF16))
    narrow = (COUNT, 16)
    tile_of = one_hot(iota(narrow, 1) == 2 * (me % 8) + (iota(narrow, 0) % MEM) // 4)
    for values in (y_in, rinv_in):
        tile = dot(tile_of, values[...])
        parts.append(jnp.where(ours & (spot == member % 4), tile, 0.0).astype(BF16))
    tall = (WIDTH, SLAB)
    at = iota(tall, 0)
    goal = (at // 128) * (2 * CUT) + ((at % 128) // BROWS) * CUT + at % CUT
    place = [one_hot(iota(tall, 1) == goal)] + [one_hot(lane[:128] == a) for a in (Y_AT, R_AT)]
    packed = dot(jnp.concatenate(parts, axis=1), jnp.concatenate(place, axis=0))
    packed = jnp.where(lane == ID_AT, jnp.concatenate([ids] * N, axis=0), packed)
    packed = jnp.where(lane == KIND_AT, jnp.concatenate([kinds] * N, axis=0), packed)
    send1[...] = slabs(packed)

    big = (COUNT, MEM * PAT)
    wide_rank = jnp.concatenate([rank[0:1]] * MEM, axis=1).astype(jnp.int32)
    choose[...] = one_hot(
        (wide_rank == iota(big, 0) // MEM) & (iota(big, 1) // PAT == iota(big, 0) % MEM)
    )
    inputs[6].wait()
    inputs[7].wait()
    send_s[...] = slabs(dot(choose[...], state[...]))

    square = (SLAB, SLAB)
    source, goal = iota(square, 0), iota(square, 1)
    plain = source == goal
    value = plain & ((goal == Y_AT) | (goal == R_AT))
    turn = me // 8
    mix = jnp.concatenate(
        [
            one_hot(
                (plain & ((goal < OWN) | (goal == ID_AT) | (goal == KIND_AT)))
                | (value & (turn == 0))
            ),
            one_hot(
                ((goal >= OWN) & (goal < OWN + EDGE) & (source == goal - EDGE))
                | (value & (turn == 1))
            ),
            one_hot(
                ((goal >= OWN + EDGE) & (goal < Y_AT) & (source == goal - OWN - EDGE))
                | (value & (turn == 2))
            ),
        ],
        axis=0,
    )

    pl.semaphore_wait(barrier, 2 * (N - 1))
    plane(send1, relay, s1_sem, r1_sem)
    plane(send_s, relay_s, sp_sem, rp_sem)
    arrived(relay, r1_sem)
    here = flat(relay)
    lower = jnp.concatenate([here[COUNT - MEM:], here[:COUNT - MEM]], axis=0)
    upper = jnp.concatenate([here[MEM:], here[:MEM]], axis=0)
    send2[...] = slabs(dot(jnp.concatenate([here, lower, upper], axis=1).astype(BF16), mix))
    column(lambda g: send2.at[g], recv2, s2_sem, r2_sem)
    arrived(relay_s, rp_sem)
    column(lambda g: relay_s.at[g], recv_s, ss_sem, rs_sem)

    arrived(recv2, r2_sem)
    held = flat(recv2)
    ids = held[:, ID_AT:ID_AT + 1].astype(jnp.int32)
    kinds = held[:, KIND_AT:KIND_AT + 1]
    held = held.astype(BF16)
    low, high = ids < HB, ids >= HB + BLK_DOM
    inner = CUT * (ids - HB)
    column_at = jnp.where(low, OWN + CUT * ids, jnp.where(high, inner + EDGE, inner))
    value_at = jnp.where(
        low, OWN + inner + OWN, jnp.where(high, inner - OWN + 2 * OWN, inner)
    )
    values = []
    for cut in range(CUT):
        hot = one_hot(iota((COUNT, SLAB), 1) == column_at + cut)
        picked = slabs(dot_dims(hot, held, NT))
        send3[:, 2 * cut] = picked[:, :, 0:128]
        send3[:, 2 * cut + 1] = picked[:, :, 128:256]
        hot = one_hot(iota((COUNT, COUNT), 1) == value_at + cut)
        values.append(dot(hot, held))
    turned = dot(values[1].astype(BF16), one_hot(source == goal - SIDE))
    values = jnp.where(lane < Y_AT + SIDE, values[0], turned)
    send3[:, 2 * CUT] = slabs(jnp.where(lane == KIND_AT, kinds, values))
    plane(send3, recv3, s3_sem, r3_sem)

    arrived(recv3, r3_sem)
    def part(i):
        return recv3[:, i].astype(F32).reshape(COUNT, SLAB)

    obs = jnp.concatenate(
        [
            jnp.concatenate([part(2 * cut) for cut in range(CUT)], axis=0),
            jnp.concatenate([part(2 * cut + 1) for cut in range(CUT)], axis=0),
        ],
        axis=1,
    )
    transform = analyse(obs, part(2 * CUT), table_in[...], y_it, z_it)
    arrived(recv_s, rs_sem)
    members = flat(recv_s)
    mean = jnp.sum(members, axis=0, keepdims=True) / COUNT
    update = dot_dims(transform, (members - mean).astype(BF16), TN)
    send_r[...] = slabs(mean + update)
    for k in FAR_FIRST:
        to = lax.rem(me + k, N)
        remote(send_r.at[to], recv_r.at[group], sr_sem, rr_sem, served, to).start()
    home = served == group

    @pl.when(jnp.logical_not(home))
    def _():
        remote(send_r.at[me], recv_r.at[group], sr_sem, rr_sem, served, me).start()

    @pl.when(home)
    def _():
        pltpu.make_async_copy(send_r.at[me], recv_r.at[group], rr_sem).start()

    ones = jnp.ones((COUNT, NS), BF16)
    analysed = dot_dims(choose[...], ones, TN) > 0.5
    sent(send1, s1_sem)
    sent(send_s, sp_sem)
    sent(send2, s2_sem)
    sent(relay_s, ss_sem)
    sent(send3, s3_sem)
    arrived(recv_r, rr_sem)
    back = dot_dims(choose[...], flat(recv_r).astype(BF16), TN)
    out_ref[...] = jnp.where(analysed, back, state[...].astype(F32)).astype(BF16)
    sent(send_r, sr_sem)

    @pl.when(jnp.logical_not(home))
    def _():
        one = send_r.at[0]
        pltpu.make_async_copy(one, one, sr_sem).wait()


def per_device(state, obs_ens, y_obs, obs_rinv, block_list, loc_class, loc_table, patch_active):
    hbm = pl.BlockSpec(memory_space=pltpu.HBM)
    slab = pltpu.VMEM((N, MEM, NS), BF16)
    out = pl.pallas_call(
        kernel,
        out_shape=jax.ShapeDtypeStruct((MEM * PAT, NS), BF16),
        in_specs=[hbm] * 8,
        out_specs=pl.BlockSpec(memory_space=pltpu.VMEM),
        scratch_shapes=[
            pltpu.VMEM((MEM * PAT, NS), BF16),
            pltpu.VMEM((MEM, WIDTH), BF16),
            pltpu.VMEM((16, 128), BF16),
            pltpu.VMEM((16, 128), BF16),
            pltpu.VMEM((BPP, PAT), jnp.int32),
            pltpu.VMEM((BPP, PAT), jnp.int32),
            pltpu.VMEM((1, PAT), jnp.int32),
            pltpu.VMEM((1, 8), F32),
            pltpu.VMEM((N, MEM, SLAB), BF16),
            pltpu.VMEM((N, MEM, SLAB), BF16),
            slab,
            slab,
            pltpu.VMEM((N, MEM, SLAB), BF16),
            pltpu.VMEM((N, MEM, SLAB), BF16),
            slab,
            pltpu.VMEM((N, 2 * CUT + 1, MEM, SLAB), BF16),
            pltpu.VMEM((N, 2 * CUT + 1, MEM, SLAB), BF16),
            slab,
            slab,
            pltpu.VMEM((COUNT, MEM * PAT), BF16),
            pltpu.VMEM((COUNT, COUNT), F32),
            pltpu.VMEM((COUNT, COUNT), F32),
            pltpu.SemaphoreType.DMA((8,)),
        ]
        + [pltpu.SemaphoreType.DMA(())] * 12,
        compiler_params=pltpu.CompilerParams(
            collective_id=0, has_side_effects=True, vmem_limit_bytes=32 * 1024 * 1024
        ),
        cost_estimate=pl.CostEstimate(
            flops=4_000_000_000, bytes_accessed=2_000_000, transcendentals=0
        ),
    )(
        *[
            pltpu.with_memory_space_constraint(x, pltpu.HBM)
            for x in (
                state.reshape(MEM * PAT, NS), obs_ens, y_obs.reshape(16, 128),
                obs_rinv.reshape(16, 128), block_list.T, loc_class.T, patch_active[None, :],
                loc_table[None, :],
            )
        ],
    )
    return out.reshape(MEM, PAT, NS)


def solution(mesh):
    placed = (
        P("member", "domain", None),
        P("member", "domain"),
        P("domain"),
        P("domain"),
        P("domain", None),
        P("domain", None),
        P(),
        P("domain"),
    )
    return jax.shard_map(
        per_device,
        mesh=mesh,
        in_specs=placed,
        out_specs=P("member", "domain", None),
        check_vma=False,
    )
```

```python
import jax
import jax.numpy as jnp
from jax import lax
from jax.experimental import pallas as pl
from jax.experimental.pallas import tpu as pltpu
from jax.sharding import PartitionSpec as P

MESH = pl.DeviceIdType.MESH
F32 = jnp.float32
BF16 = jnp.bfloat16
N = 32
MEM = 8
NS = 256
BROWS = 64
BPP = 8
HB = 6
BLK_DOM = 32
PAT = 64
ROWS = BPP * BROWS
HALO = HB * BROWS
WIDTH = BLK_DOM * BROWS
COUNT = N * MEM
NEWTON = 6
CUT = BROWS // N
SLAB = 128
EDGE = CUT * HB
OWN = CUT * BLK_DOM
Y_AT = OWN + 2 * EDGE
R_AT, ID_AT, KIND_AT = Y_AT + 1, Y_AT + 2, Y_AT + 3
SIDE = 16
FAR_FIRST = [16] + [s for k in range(15, 0, -1) for s in (k, N - k)]
STEPS = (0, 1, 2, 1)
PLANE = sorted(range(1, N), key=lambda k: -STEPS[k // 8] - STEPS[k % 8 // 2])
NT = (((1,), (1,)), ((), ()))
TN = (((0,), (0,)), ((), ()))


def iota(shape, dim):
    return lax.broadcasted_iota(jnp.int32, shape, dim)


def dot(a, b):
    return jnp.dot(a, b, preferred_element_type=F32)


def split(a):
    high = a.astype(BF16)
    return high, (a - high.astype(F32)).astype(BF16)


def dot_dims(a, b, dims):
    return lax.dot_general(a, b, dims, preferred_element_type=F32)


def dot3(a, b, dims=(((1,), (0,)), ((), ()))):
    return dot_dims(a[0], b[0], dims) + (dot_dims(a[0], b[1], dims) + dot_dims(a[1], b[0], dims))


def one_hot(condition):
    return condition.astype(F32).astype(BF16)


def flat(ref):
    value = ref[...].astype(F32)
    return value.reshape(value.shape[0] * value.shape[1], value.shape[2])


def slabs(value):
    return value.reshape(N, MEM, value.shape[-1]).astype(BF16)


def analyse(obs, values, table, y_it, z_it, beside):
    def column_of(at, step):
        return jnp.concatenate([values[:, at + step * k:at + step * k + 1] for k in range(CUT)], 0)

    mean = dot(obs.astype(BF16), jnp.ones((COUNT, COUNT), BF16)) / COUNT
    pert = (obs - mean).astype(BF16)
    kind = column_of(KIND_AT, 0)
    local = jnp.zeros(kind.shape, F32)
    for c in range(8):
        local = jnp.where(kind == c, table[:, c:c + 1], local)
    weight = column_of(R_AT, SIDE) * local
    weighted = (pert.astype(F32) * weight).astype(BF16)
    gram = dot_dims(weighted, pert, TN)
    eye = (iota((COUNT, COUNT), 0) == iota((COUNT, COUNT), 1)).astype(F32)
    system = eye + gram / (COUNT - 1)
    innovation = column_of(Y_AT, SIDE) - mean
    projected = jnp.sum(weighted.astype(F32) * innovation, axis=0, keepdims=True)
    squares = jnp.sum(jnp.sum(system * system, axis=0, keepdims=True), axis=1, keepdims=True)
    fro = jnp.sqrt(squares)
    first = system / fro
    half = 1.5 * eye - 0.5 * first
    y_it[...] = dot3(split(first), split(half))
    z_it[...] = half

    def step(_, carry):
        y, z = split(y_it[...]), split(z_it[...])
        middle = split(1.5 * eye - 0.5 * dot3(z, y))
        y_it[...] = dot3(y, middle)
        z_it[...] = dot3(middle, z)
        return carry

    lax.fori_loop(0, NEWTON - 2, step, 0)
    other = beside()
    y, z = split(y_it[...]), split(z_it[...])
    last = dot3(split(1.5 * eye - 0.5 * dot3(z, y)), z)
    z = split(last)
    inner = dot3(z, split(jnp.broadcast_to(projected, (128, COUNT))), NT)
    shift = dot3(z, split(inner)) / (fro * (COUNT - 1))
    shift = jnp.concatenate([shift, shift], axis=1)
    return (last / jnp.sqrt(fro) + shift).astype(BF16), other


def level(group):
    return group // 2 + (N // 2) * (group % 2)


def group_of(lev):
    return 2 * (lev % (N // 2)) + lev // (N // 2)


def ranks(active):
    square = (PAT, PAT)
    upto = (iota(square, 0) <= iota(square, 1)).astype(F32)
    return jnp.where(active > 0.5, dot(active, upto) - 1.0, -1.0)


def kernel(
    state_hbm, obs_hbm, y_hbm, rinv_hbm, list_hbm, class_hbm, active_hbm, table_hbm, out_ref,
    state, obs_in, y_in, rinv_in, list_in, class_in, active_in, table_in,
    send1, relay, send_s, relay_s, send2, recv2, recv_s, send3, recv3, send_r, recv_r, choose, back_to, y_it, z_it,
    in_sem, s1_sem, r1_sem, sp_sem, rp_sem, s2_sem, r2_sem, ss_sem, rs_sem, s3_sem, r3_sem, sr_sem, rr_sem,
):
    group, me = lax.axis_index("domain"), lax.axis_index("member")
    served = group_of(me)

    inputs = [
        pltpu.make_async_copy(src, dst, in_sem.at[i])
        for i, (src, dst) in enumerate(
            [
                (active_hbm, active_in),
                (list_hbm, list_in),
                (class_hbm, class_in),
                (y_hbm, y_in),
                (rinv_hbm, rinv_in),
                (obs_hbm, obs_in),
                (state_hbm, state),
                (table_hbm, table_in),
            ]
        )
    ]
    for copy in inputs:
        copy.start()

    barrier = pltpu.get_barrier_semaphore()
    for k in FAR_FIRST:
        to = {"domain": group, "member": lax.rem(me + k, N)}
        pl.semaphore_signal(barrier, inc=1, device_id=to, device_id_type=MESH)
    for k in range(1, N):
        to = {"domain": lax.rem(group + k, N), "member": me}
        pl.semaphore_signal(barrier, inc=1, device_id=to, device_id_type=MESH)

    def remote(src, dst, send_sem, recv_sem, dom, mem):
        return pltpu.make_async_remote_copy(
            src_ref=src, dst_ref=dst, send_sem=send_sem, recv_sem=recv_sem,
            device_id={"domain": dom, "member": mem}, device_id_type=MESH,
        )

    def arrived(dst, recv_sem):
        pltpu.make_async_copy(dst, dst, recv_sem).wait()

    def sent(src, send_sem):
        part = src.at[pl.ds(0, N - 1)]
        pltpu.make_async_copy(part, part, send_sem).wait()

    def plane(src, dst, send_sem, recv_sem):
        pltpu.make_async_copy(src.at[group], dst.at[group], recv_sem).start()
        for k in PLANE:
            to = lax.rem(group + k, N)
            remote(src.at[to], dst.at[group], send_sem, recv_sem, to, me).start()

    def column(src_at, dst, send_sem, recv_sem):
        for k in FAR_FIRST:
            to = lax.rem(me + k, N)
            remote(src_at(group_of(to)), dst.at[me], send_sem, recv_sem, group, to).start()
        pltpu.make_async_copy(src_at(served), dst.at[me], recv_sem).start()

    for copy in inputs[:6]:
        copy.wait()
    active = jnp.broadcast_to(active_in[...].astype(F32), (8, PAT))
    rank = ranks(active)
    mine = rank == jnp.broadcast_to(me, (8, PAT)).astype(F32)
    local_ids = (list_in[...] - (group * BLK_DOM - HB)).astype(F32)
    ids = jnp.sum(jnp.where(mine, local_ids, 0.0), axis=1, keepdims=True)
    kinds = jnp.sum(jnp.where(mine, class_in[...].astype(F32), 0.0), axis=1, keepdims=True)

    square = (COUNT, 128)
    row, lane = iota(square, 0), iota(square, 1)
    member = row % MEM
    ours = (lane % BROWS) // CUT == row // MEM
    spot = (lane // BROWS) * CUT + lane % CUT
    obs = obs_in[...].astype(F32)
    parts = []
    for t in range(WIDTH // 128):
        tile = jnp.concatenate([obs[:, t * 128:(t + 1) * 128]] * N, axis=0)
        parts.append(jnp.where(ours, tile, 0.0).astype(BF16))
    narrow = (COUNT, 16)
    tile_of = one_hot(iota(narrow, 1) == 2 * (me % 8) + (iota(narrow, 0) % MEM) // 4)
    for values in (y_in, rinv_in):
        tile = dot(tile_of, values[...])
        for cut in range(CUT):
            wanted = member % 4 // CUT * CUT + cut
            parts.append(jnp.where(ours & (spot == wanted), tile, 0.0).astype(BF16))
    tall = (WIDTH, SLAB)
    at = iota(tall, 0)
    goal = (at // 128) * (2 * CUT) + ((at % 128) // BROWS) * CUT + at % CUT
    place = [one_hot(iota(tall, 1) == goal)] + [
        one_hot(lane[:128] == a) for a in (Y_AT, Y_AT + SIDE, R_AT, R_AT + SIDE)
    ]
    packed = dot(jnp.concatenate(parts, axis=1), jnp.concatenate(place, axis=0))
    packed = jnp.where(lane == ID_AT, jnp.concatenate([ids] * N, axis=0), packed)
    packed = jnp.where(lane == KIND_AT, jnp.concatenate([kinds] * N, axis=0), packed)
    send1[...] = slabs(packed)

    big = (COUNT, MEM * PAT)
    wide_rank = jnp.concatenate([rank[0:1]] * MEM, axis=1).astype(jnp.int32)
    choose[...] = one_hot(
        (wide_rank == iota(big, 0) // MEM) & (iota(big, 1) // PAT == iota(big, 0) % MEM)
    )
    inputs[6].wait()
    inputs[7].wait()
    send_s[...] = slabs(dot(choose[...], state[...]))

    square = (SLAB, SLAB)
    source, goal = iota(square, 0), iota(square, 1)
    plain = source == goal
    value = plain & ((goal == Y_AT) | (goal == R_AT) | (goal >= Y_AT + SIDE))
    turn = me // 8
    mix = jnp.concatenate(
        [
            one_hot(
                (plain & ((goal < OWN) | (goal == ID_AT) | (goal == KIND_AT)))
                | (value & (turn == 0))
            ),
            one_hot(
                ((goal >= OWN) & (goal < OWN + EDGE) & (source == goal - EDGE))
                | (value & (turn == 1))
            ),
            one_hot(
                ((goal >= OWN + EDGE) & (goal < Y_AT) & (source == goal - OWN - EDGE))
                | (value & (turn == 2))
            ),
        ],
        axis=0,
    )

    pl.semaphore_wait(barrier, 2 * (N - 1))
    plane(send1, relay, s1_sem, r1_sem)
    plane(send_s, relay_s, sp_sem, rp_sem)
    arrived(relay, r1_sem)
    here = flat(relay)
    lower = jnp.concatenate([here[COUNT - MEM:], here[:COUNT - MEM]], axis=0)
    upper = jnp.concatenate([here[MEM:], here[:MEM]], axis=0)
    send2[...] = slabs(dot(jnp.concatenate([here, lower, upper], axis=1).astype(BF16), mix))
    column(lambda g: send2.at[g], recv2, s2_sem, r2_sem)
    arrived(relay_s, rp_sem)
    column(lambda g: relay_s.at[g], recv_s, ss_sem, rs_sem)

    arrived(recv2, r2_sem)
    held = flat(recv2)
    ids = held[:, ID_AT:ID_AT + 1].astype(jnp.int32)
    kinds = held[:, KIND_AT:KIND_AT + 1]
    held = held.astype(BF16)
    low, high = ids < HB, ids >= HB + BLK_DOM
    inner = CUT * (ids - HB)
    column_at = jnp.where(low, OWN + CUT * ids, jnp.where(high, inner + EDGE, inner))
    value_at = jnp.where(
        low, OWN + inner + OWN, jnp.where(high, inner - OWN + 2 * OWN, inner)
    )
    for cut in range(CUT):
        hot = one_hot(iota((COUNT, SLAB), 1) == column_at + cut)
        picked = slabs(dot_dims(hot, held, NT))
        send3[:, 2 * cut] = picked[:, :, 0:128]
        send3[:, 2 * cut + 1] = picked[:, :, 128:256]
    values = dot(one_hot(iota((COUNT, COUNT), 1) == value_at), held)
    send3[:, 2 * CUT] = slabs(jnp.where(lane == KIND_AT, kinds, values))
    plane(send3, recv3, s3_sem, r3_sem)

    arrived(recv3, r3_sem)
    def part(i):
        return recv3[:, i].astype(F32).reshape(COUNT, SLAB)

    obs = jnp.concatenate(
        [
            jnp.concatenate([part(2 * cut) for cut in range(CUT)], axis=0),
            jnp.concatenate([part(2 * cut + 1) for cut in range(CUT)], axis=0),
        ],
        axis=1,
    )
    def centred():
        arrived(recv_s, rs_sem)
        members = flat(recv_s)
        mean = jnp.sum(members, axis=0, keepdims=True) / COUNT
        return mean, (members - mean).astype(BF16)

    transform, (mean, pert) = analyse(obs, part(2 * CUT), table_in[...], y_it, z_it, centred)
    update = dot_dims(transform, pert, TN)
    send_r[...] = slabs(mean + update)
    for k in FAR_FIRST:
        to = lax.rem(me + k, N)
        remote(send_r.at[to], recv_r.at[group], sr_sem, rr_sem, served, to).start()
    home = served == group

    @pl.when(jnp.logical_not(home))
    def _():
        remote(send_r.at[me], recv_r.at[group], sr_sem, rr_sem, served, me).start()

    @pl.when(home)
    def _():
        pltpu.make_async_copy(send_r.at[me], recv_r.at[group], rr_sem).start()

    ones = jnp.ones((COUNT, NS), BF16)
    analysed = dot_dims(choose[...], ones, TN) > 0.5
    eye = one_hot(iota((COUNT, COUNT), 0) == iota((COUNT, COUNT), 1))
    back_to[...] = dot_dims(choose[...], eye, TN).astype(BF16)
    out_ref[...] = jnp.where(analysed, 0.0, state[...].astype(F32)).astype(BF16)
    sent(send1, s1_sem)
    sent(send_s, sp_sem)
    sent(send2, s2_sem)
    sent(relay_s, ss_sem)
    sent(send3, s3_sem)
    arrived(recv_r, rr_sem)
    back = dot(back_to[...], flat(recv_r).astype(BF16))
    out_ref[...] = (out_ref[...].astype(F32) + back).astype(BF16)
    sent(send_r, sr_sem)

    @pl.when(jnp.logical_not(home))
    def _():
        one = send_r.at[0]
        pltpu.make_async_copy(one, one, sr_sem).wait()


def per_device(state, obs_ens, y_obs, obs_rinv, block_list, loc_class, loc_table, patch_active):
    hbm = pl.BlockSpec(memory_space=pltpu.HBM)
    slab = pltpu.VMEM((N, MEM, NS), BF16)
    out = pl.pallas_call(
        kernel,
        out_shape=jax.ShapeDtypeStruct((MEM * PAT, NS), BF16),
        in_specs=[hbm] * 8,
        out_specs=pl.BlockSpec(memory_space=pltpu.VMEM),
        scratch_shapes=[
            pltpu.VMEM((MEM * PAT, NS), BF16),
            pltpu.VMEM((MEM, WIDTH), BF16),
            pltpu.VMEM((16, 128), BF16),
            pltpu.VMEM((16, 128), BF16),
            pltpu.VMEM((BPP, PAT), jnp.int32),
            pltpu.VMEM((BPP, PAT), jnp.int32),
            pltpu.VMEM((1, PAT), jnp.int32),
            pltpu.VMEM((1, 8), F32),
            pltpu.VMEM((N, MEM, SLAB), BF16),
            pltpu.VMEM((N, MEM, SLAB), BF16),
            slab,
            slab,
            pltpu.VMEM((N, MEM, SLAB), BF16),
            pltpu.VMEM((N, MEM, SLAB), BF16),
            slab,
            pltpu.VMEM((N, 2 * CUT + 1, MEM, SLAB), BF16),
            pltpu.VMEM((N, 2 * CUT + 1, MEM, SLAB), BF16),
            slab,
            slab,
            pltpu.VMEM((COUNT, MEM * PAT), BF16),
            pltpu.VMEM((MEM * PAT, COUNT), BF16),
            pltpu.VMEM((COUNT, COUNT), F32),
            pltpu.VMEM((COUNT, COUNT), F32),
            pltpu.SemaphoreType.DMA((8,)),
        ]
        + [pltpu.SemaphoreType.DMA(())] * 12,
        compiler_params=pltpu.CompilerParams(
            collective_id=0, has_side_effects=True, vmem_limit_bytes=32 * 1024 * 1024
        ),
        cost_estimate=pl.CostEstimate(
            flops=4_000_000_000, bytes_accessed=2_000_000, transcendentals=0
        ),
    )(
        *[
            pltpu.with_memory_space_constraint(x, pltpu.HBM)
            for x in (
                state.reshape(MEM * PAT, NS), obs_ens, y_obs.reshape(16, 128),
                obs_rinv.reshape(16, 128), block_list.T, loc_class.T, patch_active[None, :],
                loc_table[None, :],
            )
        ],
    )
    return out.reshape(MEM, PAT, NS)


def solution(mesh):
    placed = (
        P("member", "domain", None),
        P("member", "domain"),
        P("domain"),
        P("domain"),
        P("domain", None),
        P("domain", None),
        P(),
        P("domain"),
    )
    return jax.shard_map(
        per_device,
        mesh=mesh,
        in_specs=placed,
        out_specs=P("member", "domain", None),
        check_vma=False,
    )
```
